512 devices in a mesh: dp: 64 (over y, z), tensor: 8 (over x, core).
Axes of the slice: x: 4, y: 8, z: 8, core: 2. Of those that a mesh axis runs over, the one named last changes fastest.
Arguments:
- input_acts: bfloat16 [16384, 8192], P('dp', 'tensor'), may hold values from -6 to 6
- hidden_acts: bfloat16 [16384, 28672], P('dp', 'tensor'), may hold values from -6 to 6
- up_grads: bfloat16 [16384, 28672], P('dp', 'tensor'), may hold values from -144 to 144
- output_grads: bfloat16 [16384, 8192], P('dp', 'tensor'), may hold values from -144 to 144
- inner_up: bfloat16 [64, 8192], P(None, 'tensor'), may hold values from -0.0625 to 0.0625
- outer_up: bfloat16 [64, 28672], P(None, 'tensor'), may hold values from -0.09449112 to 0.09449112
- inner_down: bfloat16 [64, 28672], P(None, 'tensor'), may hold values from -0.03125 to 0.03125
- outer_down: bfloat16 [64, 8192], P(None, 'tensor'), may hold values from -0.176776695 to 0.176776695
Outputs:
- logged_up: float32 [256, 4096], P('dp', 'tensor')
- logged_down: float32 [256, 4096], P('dp', 'tensor')
- fisher_up: float32 [4096, 4096], P('dp', 'tensor')
- fisher_down: float32 [4096, 4096], P('dp', 'tensor')
The draws below stay inside these ranges and needn't reach their ends.
All inputs are finite; a program needn't handle non-finite values.
Results may differ from the reference program's by a relative error of at most 0.0003.
Values sent between devices are 32-bit elements; how exact they have to be, the bound alone decides.
A program may use at most 64 MiB of HBM per device.

```python
import math
import jax
import jax.numpy as jnp
from jax import lax

D = 8192
FF = 28672
K = 64
LEN = 64
SEQS = 256
TOKENS = 16384


def sequence_scale(key, rows):
    count = rows // LEN
    order = jnp.arange(rows) // LEN
    rising = 3.0 ** (0.5 * order.astype(jnp.float32) / max(count - 1, 1))
    jitter = jnp.exp(jax.random.uniform(key, (count,), jnp.float32, -0.4, 0.4))
    return rising * jitter[order] * math.sqrt(LEN)


def row_scale(key, rows, low, high):
    return jnp.exp(jax.random.uniform(key, (rows,), jnp.float32, math.log(low), math.log(high)))


def draw_up_grads(key, part):
    key = jax.random.fold_in(key, 1)
    scales = sequence_scale(jax.random.fold_in(key, 5), TOKENS)
    values = jnp.clip(jax.random.normal(jax.random.fold_in(key, 6), (TOKENS, FF), jnp.float32), -6.0, 6.0)
    return (values * scales[:, None]).astype(jnp.bfloat16)


def draw_output_grads(key, part):
    key = jax.random.fold_in(key, 2)
    scales = sequence_scale(jax.random.fold_in(key, 5), TOKENS)
    values = jnp.clip(jax.random.normal(jax.random.fold_in(key, 6), (TOKENS, D), jnp.float32), -6.0, 6.0)
    return (values * scales[:, None]).astype(jnp.bfloat16)


def draw_outer_up(key, part):
    key = jax.random.fold_in(key, 3)
    values = jnp.clip(jax.random.normal(jax.random.fold_in(key, 5), (K, FF), jnp.float32), -4.0, 4.0)
    scales = row_scale(jax.random.fold_in(key, 6), K, 0.5, 3.0)
    return (values * scales[:, None] / math.sqrt(FF)).astype(jnp.bfloat16)


def draw_outer_down(key, part):
    key = jax.random.fold_in(key, 4)
    values = jnp.clip(jax.random.normal(jax.random.fold_in(key, 5), (K, D), jnp.float32), -4.0, 4.0)
    scales = row_scale(jax.random.fold_in(key, 6), K, 0.5, 3.0)
    return (values * scales[:, None] / math.sqrt(D)).astype(jnp.bfloat16)


def block_scale(stream_key, dims, cuts, low, high):
    def one(position, parts):
        heights = jax.random.uniform(jax.random.fold_in(jax.random.fold_in(stream_key, 6), position), (parts,), jnp.float32, low / len(cuts), high / len(cuts))
        return jnp.repeat(jnp.exp(heights), dims[position] // parts).reshape((-1,) + (1,) * (len(dims) - position - 1))

    factor_of = one(*cuts[0])
    for cut in cuts[1:]:
        factor_of = factor_of * one(*cut)
    return factor_of


def normal_values(rng, shape, spread, most, cuts=(), held_as=jnp.bfloat16):
    values = jax.random.normal(rng, shape, jnp.float32) * spread
    if len(cuts) > 0:
        values = block_scale(rng, shape, cuts, -0.22, 0.18) * values
    return jnp.clip(values, min=-most, max=most).astype(held_as)


def setup_inputs(seed: int = 0) -> dict:
    keys = jax.random.split(jax.random.key(seed), 9)
    input_acts = normal_values(keys[0], (TOKENS, D), 1.0, 6.0, ((0, 64), (1, 8)))
    hidden_acts = normal_values(keys[1], (TOKENS, FF), 1.0, 6.0, ((0, 64), (1, 8)))
    up_grads = draw_up_grads(jax.random.fold_in(keys[8], 71), 0)
    output_grads = draw_output_grads(jax.random.fold_in(keys[8], 71), 0)
    inner_up = normal_values(keys[4], (K, D), D ** -0.5, 0.0625, ((1, 8),))
    outer_up = draw_outer_up(jax.random.fold_in(keys[8], 71), 0)
    inner_down = normal_values(keys[6], (K, FF), FF ** -0.5, 0.03125, ((1, 8),))
    outer_down = draw_outer_down(jax.random.fold_in(keys[8], 71), 0)
    return {"input_acts": input_acts, "hidden_acts": hidden_acts, "up_grads": up_grads, "output_grads": output_grads, "inner_up": inner_up, "outer_up": outer_up, "inner_down": inner_down, "outer_down": outer_down}


DAMPING = 0.5


def project(acts, basis):
    return jnp.dot(acts, basis.T, preferred_element_type=jnp.float32)


def per_sequence(grads, acts):
    grad_blocks = grads.reshape(SEQS, LEN, K)
    act_blocks = acts.reshape(SEQS, LEN, K)
    outer = jnp.einsum("slk,slm->skm", grad_blocks, act_blocks, precision=lax.Precision.HIGHEST) / LEN
    return outer.reshape(SEQS, K * K)


def damped_fisher(logged):
    trace = jnp.sum(logged * logged) / SEQS
    gram = jnp.dot(logged.T, logged, precision=lax.Precision.HIGHEST) / SEQS
    return gram + (DAMPING * trace / (K * K)) * jnp.eye(K * K, dtype=jnp.float32)


def reference(input_acts, hidden_acts, up_grads, output_grads, inner_up, outer_up, inner_down, outer_down):
    act_up = project(input_acts, inner_up)
    grad_up = project(up_grads, outer_up)
    act_down = project(hidden_acts, inner_down)
    grad_down = project(output_grads, outer_down)
    logged_up = per_sequence(grad_up, act_up)
    logged_down = per_sequence(grad_down, act_down)
    return logged_up, logged_down, damped_fisher(logged_up), damped_fisher(logged_down)
```

```python
import functools

import jax
import jax.numpy as jnp
from jax import lax
from jax.experimental import pallas as pl
from jax.experimental.pallas import tpu as pltpu
from jax.sharding import PartitionSpec as P

LEN = 64
DAMPING = 0.5
WIDTH = 64
NT = 8
NY = 8
NZ = 8
SEQS = 256
FLAT = WIDTH * WIDTH
COLS = FLAT // NT
HALF = COLS // 2
LOADS = 4
MESH = pl.DeviceIdType.MESH
HIGHEST = lax.Precision.HIGHEST


def project(acts, basis):
    return lax.dot_general(
        acts, basis, (((1,), (1,)), ((), ())), preferred_element_type=jnp.float32
    )


def contract_rows(left, right):
    return lax.dot_general(
        left,
        right,
        (((0,), (0,)), ((), ())),
        precision=HIGHEST,
        preferred_element_type=jnp.float32,
    )


def kernel(
    ia, ha, ug, og, iu, ou, idn, od,
    log_up, log_dn, f_up, f_dn,
    x_ia, x_ha, x_ug, x_og, w_iu, w_ou, w_id, w_od,
    part, rs, mpad, a2a, ly, lz, lbuf, lp, ra, rb,
    load_sem,
    rs_s, rs_r, a2a_s, a2a_r, ly_s, ly_r, lz_s, lz_r, lt_s, lt_r,
    p1a_s, p1a_r, p1b_s, p1b_r, p2_s, p2_r,
):
    t = lax.axis_index("tensor")
    r = lax.axis_index("dp")
    y = r // NZ
    z = r % NZ

    def at_t(d):
        return (t + d) % NT

    def at_y(d):
        return (y + d) % NY

    def at_z(d):
        return (z + d) % NZ

    def remote(src, dst, send, recv, dp, tensor):
        return pltpu.make_async_remote_copy(
            src_ref=src,
            dst_ref=dst,
            send_sem=send,
            recv_sem=recv,
            device_id=(dp, tensor),
            device_id_type=MESH,
        )

    barrier = pltpu.get_barrier_semaphore()
    for d in range(1, NT):
        pl.semaphore_signal(barrier, inc=1, device_id=(r, at_t(d)), device_id_type=MESH)
    for d in range(1, NY):
        pl.semaphore_signal(barrier, inc=1, device_id=(at_y(d) * NZ + z, t), device_id_type=MESH)
    for d in range(1, NZ):
        pl.semaphore_signal(barrier, inc=1, device_id=(y * NZ + at_z(d), t), device_id_type=MESH)

    wide = ug.shape[1]
    piece = wide // LOADS
    loads = []

    def load(src, dst):
        copy = pltpu.make_async_copy(src, dst, load_sem.at[len(loads)])
        copy.start()
        loads.append(copy)
        return copy

    def wide_loads(src, dst):
        return [
            load(src.at[:, pl.ds(c * piece, piece)], dst.at[:, pl.ds(c * piece, piece)])
            for c in range(LOADS)
        ]

    up_narrow = [load(iu, w_iu), load(ia, x_ia)]
    up_basis = load(ou, w_ou)
    up_wide = wide_loads(ug, x_ug)
    dn_narrow = [load(od, w_od), load(og, x_og)]
    dn_basis = load(idn, w_id)
    dn_wide = wide_loads(ha, x_ha)

    def projected(narrow, basis, wides, x_n, w_n, x_w, w_w):
        for copy in narrow:
            copy.wait()
        slim = project(x_n[...], w_n[...])
        basis.wait()
        total = None
        for c, copy in enumerate(wides):
            copy.wait()
            cut = slice(c * piece, (c + 1) * piece)
            term = project(x_w[:, cut], w_w[:, cut])
            total = term if total is None else total + term
        return slim, total

    def scatter(first):
        for m in range(first, first + NT // 2):

            @pl.when(t != m)
            def _():
                remote(part.at[m], rs.at[t], rs_s.at[m], rs_r.at[t], r, m).start()

    act, grad = projected(up_narrow, up_basis, up_wide, x_ia, w_iu, x_ug, w_ou)
    part[0 : NT // 2] = jnp.concatenate([act, grad], axis=1).reshape(NT // 2, LEN, 2 * WIDTH)
    pl.semaphore_wait(barrier, (NT - 1) + (NY - 1) + (NZ - 1))
    scatter(0)
    grad, act = projected(dn_narrow, dn_basis, dn_wide, x_og, w_od, x_ha, w_id)
    part[NT // 2 :] = jnp.concatenate([act, grad], axis=1).reshape(NT // 2, LEN, 2 * WIDTH)
    scatter(NT // 2)

    total = part[t]
    for d in range(1, NT):
        src = at_t(d)
        remote(rs.at[src], rs.at[src], rs_s.at[src], rs_r.at[src], r, src).wait_recv()
        total = total + rs[src]
    outer = contract_rows(total, total)[WIDTH:] * (1.0 / LEN)
    lanes = lax.broadcasted_iota(jnp.int32, (WIDTH, 2 * WIDTH), 1)
    squares = jnp.sum(outer * outer, axis=0, keepdims=True)
    squares = pltpu.roll(jnp.broadcast_to(squares, (8, 2 * WIDTH)), WIDTH, 1)
    squares = jnp.broadcast_to(squares[0:1], (WIDTH, 2 * WIDTH))
    mpad[...] = jnp.where(lanes < WIDTH, outer, squares)

    def rows8(i):
        return pl.ds(pl.multiple_of(i * 8, 8), 8)

    for d in range(1, NT):
        to = at_t(d)
        remote(
            mpad.at[rows8(to)], a2a.at[rows8(t)], a2a_s.at[d], a2a_r.at[t], r, to
        ).start()
    for d in range(1, NY):
        to = at_y(d)
        remote(
            mpad.at[rows8(to)], ly.at[rows8(y)], ly_s.at[d], ly_r.at[y], to * NZ + z, t
        ).start()
    a2a[rows8(t), :] = mpad[rows8(t), :]
    ly[rows8(y), :] = mpad[rows8(y), :]

    for d in range(1, NT):
        src = at_t(d)
        remote(
            a2a.at[rows8(src)], a2a.at[rows8(src)], a2a_s.at[d], a2a_r.at[src], r, src
        ).wait_recv()
    lane8 = lax.broadcasted_iota(jnp.int32, (8, 2 * WIDTH), 1)
    sub8 = lax.broadcasted_iota(jnp.int32, (8, 2 * WIDTH), 0)
    for k in range(4):
        even = a2a[pl.ds(2 * k, 8, stride=8), :]
        odd = a2a[pl.ds(2 * k + 1, 8, stride=8), :]
        tile = jnp.where(lane8 < WIDTH, even, pltpu.roll(odd, WIDTH, 1))
        log_up[:, k * 128 : (k + 1) * 128] = tile[0:4]
        log_dn[:, k * 128 : (k + 1) * 128] = tile[4:8]
        half = ra if k < 2 else rb
        half[z, y, :, (k % 2) * 128 : (k % 2 + 1) * 128] = tile

    for d in range(1, NZ):
        to = at_z(d)
        remote(
            ra.at[z, y], ra.at[z, y], p1a_s.at[d], p1a_r.at[z], y * NZ + to, t
        ).start()
        to = at_y(d)
        remote(
            rb.at[z, y], rb.at[z, y], p1b_s.at[d], p1b_r.at[y], to * NZ + z, t
        ).start()

    for d in range(1, NY):
        src = at_y(d)
        remote(
            ly.at[rows8(src)], ly.at[rows8(src)], ly_s.at[d], ly_r.at[src], src * NZ + z, t
        ).wait_recv()
    for i in range(NZ):
        lz[i] = ly[pl.ds(i, 8, stride=8), :]
    for d in range(1, NZ):
        to = at_z(d)
        slot = pl.ds(pl.multiple_of(t * 64 + z * 8, 8), 8)
        remote(lz.at[to], lbuf.at[slot], lz_s.at[d], lz_r.at[z], y * NZ + to, t).start()
    lbuf[pl.ds(pl.multiple_of(t * 64 + z * 8, 8), 8), :] = lz[z]

    def leg(h, way, step, c):
        sign = 1 if way == 0 else -1
        if h == 0:
            origin = at_y(-sign * step + NY)
            ref = ra.at[pl.ds(4 * c, 4), origin]
            dp = at_y(sign + NY) * NZ + z
        else:
            origin = at_z(-sign * step + NZ)
            ref = rb.at[origin, pl.ds(4 * c, 4)]
            dp = y * NZ + at_z(sign + NZ)
        index = ((h * 2 + way) * 4 + step) * 2 + c
        return remote(ref, ref, p2_s.at[index], p2_r.at[index], dp, t)

    def arrived(h, way, step, c):
        sign = 1 if way == 0 else -1
        if h == 0:
            origin = at_y(-sign * (step + 1) + NY)
            ref = ra.at[pl.ds(4 * c, 4), origin]
        else:
            origin = at_z(-sign * (step + 1) + NZ)
            ref = rb.at[origin, pl.ds(4 * c, 4)]
        index = ((h * 2 + way) * 4 + step) * 2 + c
        remote(ref, ref, p2_s.at[index], p2_r.at[index], r, t).wait_recv()

    def runs(way, step, c):
        return step < 3 or c == way

    for d in range(1, NZ):
        src = at_z(d)
        remote(
            ra.at[src, y], ra.at[src, y], p1a_s.at[d], p1a_r.at[src], r, t
        ).wait_recv()
        src = at_y(d)
        remote(
            rb.at[z, src], rb.at[z, src], p1b_s.at[d], p1b_r.at[src], r, t
        ).wait_recv()
    for c in range(2):
        for h in range(2):
            for way in range(2):
                leg(h, way, 0, c).start()

    for d in range(1, NZ):
        src = at_z(d)
        slot = pl.ds(pl.multiple_of(t * 64 + src * 8, 8), 8)
        remote(lbuf.at[slot], lbuf.at[slot], lz_s.at[d], lz_r.at[src], r, t).wait_recv()

    def rows64(i):
        return pl.ds(pl.multiple_of(i * 64, 64), 64)

    for d in range(1, NT):
        remote(
            lbuf.at[rows64(t)], lbuf.at[rows64(t)], lt_s.at[d], lt_r.at[t], r, at_t(d)
        ).start()

    for step in range(1, 4):
        for c in range(2):
            for h in range(2):
                for way in range(2):
                    arrived(h, way, step - 1, c)
                    if runs(way, step, c):
                        leg(h, way, step, c).start()

    for d in range(1, NT):
        src = at_t(d)
        remote(
            lbuf.at[rows64(src)], lbuf.at[rows64(src)], lt_s.at[d], lt_r.at[src], r, t
        ).wait_recv()
    tally = jnp.zeros((8, 2 * WIDTH), jnp.float32)
    for i in range(NY * NZ):
        tile = lbuf[pl.ds(i, 8, stride=64), :]
        tally = tally + tile
        low = jnp.where((sub8 < 4) & (lane8 < WIDTH), tile, 0.0)
        high = jnp.where((sub8 >= 4) & (lane8 >= WIDTH), pltpu.roll(tile, WIDTH, 1), 0.0)
        lp[i * 8 : (i + 1) * 8, :] = low + high
    tally = jnp.where(lane8 >= WIDTH, tally, 0.0)
    trace_up = jnp.sum(jnp.where(sub8 < 4, tally, 0.0)) / SEQS
    trace_dn = jnp.sum(jnp.where(sub8 >= 4, tally, 0.0)) / SEQS

    row_ids = r * WIDTH + lax.broadcasted_iota(jnp.int32, (WIDTH, HALF), 0)
    col_ids = t * COLS + lax.broadcasted_iota(jnp.int32, (WIDTH, HALF), 1)
    for h in range(2):
        for way in range(2):
            arrived(h, way, 3, way)
        half = ra if h == 0 else rb
        gram = contract_rows(lp[...], half[...].reshape(8 * NY * NZ, HALF)) * (1.0 / SEQS)
        same = row_ids == col_ids + h * HALF
        cut = slice(h * HALF, (h + 1) * HALF)
        f_up[:, cut] = gram[:WIDTH] + jnp.where(same, DAMPING * trace_up / FLAT, 0.0)
        f_dn[:, cut] = gram[WIDTH:] + jnp.where(same, DAMPING * trace_dn / FLAT, 0.0)

    for m in range(NT):

        @pl.when(t != m)
        def _():
            remote(part.at[m], rs.at[t], rs_s.at[m], rs_r.at[t], r, m).wait_send()

    for d in range(1, NT):
        to = at_t(d)
        remote(mpad.at[rows8(to)], a2a.at[rows8(t)], a2a_s.at[d], a2a_r.at[t], r, to).wait_send()
        to = at_y(d)
        remote(mpad.at[rows8(to)], ly.at[rows8(y)], ly_s.at[d], ly_r.at[y], r, t).wait_send()
        to = at_z(d)
        remote(lz.at[to], lbuf.at[rows8(z)], lz_s.at[d], lz_r.at[z], r, t).wait_send()
        remote(lbuf.at[rows64(t)], lbuf.at[rows64(t)], lt_s.at[d], lt_r.at[t], r, t).wait_send()
        remote(ra.at[z, y], ra.at[z, y], p1a_s.at[d], p1a_r.at[z], r, t).wait_send()
        remote(rb.at[z, y], rb.at[z, y], p1b_s.at[d], p1b_r.at[y], r, t).wait_send()
    for step in range(4):
        for c in range(2):
            for h in range(2):
                for way in range(2):
                    if runs(way, step, c):
                        leg(h, way, step, c).wait_send()


def body(
    input_acts, hidden_acts, up_grads, output_grads, inner_up, outer_up, inner_down, outer_down
):
    operands = (
        input_acts,
        hidden_acts,
        up_grads,
        output_grads,
        inner_up,
        outer_up,
        inner_down,
        outer_down,
    )
    f32 = jnp.float32
    dma = pltpu.SemaphoreType.DMA
    return pl.pallas_call(
        kernel,
        out_shape=(
            jax.ShapeDtypeStruct((NT // 2, COLS), f32),
            jax.ShapeDtypeStruct((NT // 2, COLS), f32),
            jax.ShapeDtypeStruct((WIDTH, COLS), f32),
            jax.ShapeDtypeStruct((WIDTH, COLS), f32),
        ),
        in_specs=[pl.BlockSpec(memory_space=pl.ANY)] * 8,
        out_specs=[pl.BlockSpec(memory_space=pltpu.VMEM)] * 4,
        scratch_shapes=[pltpu.VMEM(a.shape, a.dtype) for a in operands]
        + [
            pltpu.VMEM((NT, LEN, 2 * WIDTH), f32),
            pltpu.VMEM((NT, LEN, 2 * WIDTH), f32),
            pltpu.VMEM((WIDTH, 2 * WIDTH), f32),
            pltpu.VMEM((8 * NT, 2 * WIDTH), f32),
            pltpu.VMEM((8 * NY, 2 * WIDTH), f32),
            pltpu.VMEM((NZ, NY, 2 * WIDTH), f32),
            pltpu.VMEM((NT * NZ * NY, 2 * WIDTH), f32),
            pltpu.VMEM((NT * NZ * NY, 2 * WIDTH), f32),
            pltpu.VMEM((NZ, NY, 8, HALF), f32),
            pltpu.VMEM((NZ, NY, 8, HALF), f32),
            dma((6 + 2 * LOADS,)),
        ]
        + [dma((8,))] * 14
        + [dma((32,))] * 2,
        compiler_params=pltpu.CompilerParams(
            collective_id=0, has_side_effects=True, vmem_limit_bytes=63 * 1024 * 1024
        ),
        cost_estimate=pl.CostEstimate(
            flops=2 * 256 * 64 * 9216, bytes_accessed=6 * 1024 * 1024, transcendentals=0
        ),
    )(*operands)


def solution(mesh):
    split = P("dp", "tensor")
    basis = P(None, "tensor")
    return jax.shard_map(
        body,
        mesh=mesh,
        in_specs=(split,) * 4 + (basis,) * 4,
        out_specs=(split,) * 4,
        check_vma=False,
    )
```

```python
import jax
import jax.numpy as jnp
from jax import lax
from jax.experimental import pallas as pl
from jax.experimental.pallas import tpu as pltpu
from jax.sharding import PartitionSpec as P

LEN = 64
DAMPING = 0.5
WIDTH = 64
NT = 8
NY = 8
NZ = 8
SEQS = 256
FLAT = WIDTH * WIDTH
COLS = FLAT // NT
HALF = COLS // 2
LOADS = 4
MESH = pl.DeviceIdType.MESH


def project(acts, basis):
    return lax.dot_general(
        acts, basis, (((1,), (1,)), ((), ())), preferred_element_type=jnp.float32
    )


def contract_rows(left, right):
    def split(values):
        high = values.astype(jnp.bfloat16)
        return high, (values - high.astype(jnp.float32)).astype(jnp.bfloat16)

    def dot(a, b):
        return lax.dot_general(
            a, b, (((0,), (0,)), ((), ())), preferred_element_type=jnp.float32
        )

    left_high, left_low = split(left)
    right_high, right_low = split(right)
    cross = dot(left_high, right_low) + dot(left_low, right_high)
    return cross + dot(left_high, right_high)


def kernel(
    ia, ha, ug, og, iu, ou, idn, od,
    log_up, log_dn, f_up, f_dn,
    x_ia, x_ha, x_ug, x_og, w_iu, w_ou, w_id, w_od,
    part, rs, mpad, a2a, ly, lz, lbuf, lp, ra, rb,
    v_lu, v_ld, v_fu, v_fd,
    load_sem, out_sem,
    rs_s, rs_r, a2a_s, a2a_r, ly_s, ly_r, lz_s, lz_r, lt_s, lt_r,
    p1a_s, p1a_r, p1b_s, p1b_r, p2_s, p2_r,
):
    t = lax.axis_index("tensor")
    r = lax.axis_index("dp")
    y = r // NZ
    z = r % NZ

    def at_t(d):
        return (t + d) % NT

    def at_y(d):
        return (y + d) % NY

    def at_z(d):
        return (z + d) % NZ

    def remote(src, dst, send, recv, dp, tensor):
        return pltpu.make_async_remote_copy(
            src_ref=src,
            dst_ref=dst,
            send_sem=send,
            recv_sem=recv,
            device_id=(dp, tensor),
            device_id_type=MESH,
        )

    started = []

    def send(*copy_of):
        copy = remote(*copy_of)
        copy.start()
        started.append(copy)

    writes = []

    def write(src, dst):
        copy = pltpu.make_async_copy(src, dst, out_sem.at[len(writes)])
        copy.start()
        writes.append(copy)

    def finish():
        for m in range(NT):

            @pl.when(t != m)
            def _():
                remote(part.at[m], rs.at[t], rs_s.at[m], rs_r.at[t], r, m).wait_send()

        for copy in started:
            copy.wait_send()

    wide = ug.shape[1]
    piece = wide // LOADS
    loads = []

    def load(src, dst):
        copy = pltpu.make_async_copy(src, dst, load_sem.at[len(loads)])
        copy.start()
        loads.append(copy)
        return copy

    def wide_loads(src, dst):
        return [
            load(src.at[:, pl.ds(c * piece, piece)], dst.at[:, pl.ds(c * piece, piece)])
            for c in range(LOADS)
        ]

    up_narrow = [load(iu, w_iu), load(ia, x_ia)]
    up_basis = load(ou, w_ou)
    up_wide = wide_loads(ug, x_ug)

    barrier = pltpu.get_barrier_semaphore()
    for d in range(1, NT):
        pl.semaphore_signal(barrier, inc=1, device_id=(r, at_t(d)), device_id_type=MESH)
    for d in range(1, NY):
        pl.semaphore_signal(barrier, inc=1, device_id=(at_y(d) * NZ + z, t), device_id_type=MESH)
    for d in range(1, NZ):
        pl.semaphore_signal(barrier, inc=1, device_id=(y * NZ + at_z(d), t), device_id_type=MESH)

    def projected(narrow, basis, wides, x_n, w_n, x_w, w_w):
        for copy in narrow:
            copy.wait()
        slim = project(x_n[...], w_n[...])
        basis.wait()
        total = None
        for c, copy in enumerate(wides):
            copy.wait()
            cut = slice(c * piece, (c + 1) * piece)
            term = project(x_w[:, cut], w_w[:, cut])
            total = term if total is None else total + term
        return slim, total

    def scatter(first):
        for m in range(first, first + NT // 2):

            @pl.when(t != m)
            def _():
                remote(part.at[m], rs.at[t], rs_s.at[m], rs_r.at[t], r, m).start()

    for copy in up_narrow:
        copy.wait()
    dn_narrow = [load(od, w_od), load(og, x_og)]
    dn_basis = load(idn, w_id)
    dn_wide = wide_loads(ha, x_ha)
    act, grad = projected([], up_basis, up_wide, x_ia, w_iu, x_ug, w_ou)
    part[0 : NT // 2] = jnp.concatenate([act, grad], axis=1).reshape(NT // 2, LEN, 2 * WIDTH)
    pl.semaphore_wait(barrier, (NT - 1) + (NY - 1) + (NZ - 1))
    scatter(0)
    grad, act = projected(dn_narrow, dn_basis, dn_wide, x_og, w_od, x_ha, w_id)
    part[NT // 2 :] = jnp.concatenate([act, grad], axis=1).reshape(NT // 2, LEN, 2 * WIDTH)
    scatter(NT // 2)

    total = part[t]
    for d in range(1, NT):
        src = at_t(d)
        remote(rs.at[src], rs.at[src], rs_s.at[src], rs_r.at[src], r, src).wait_recv()
        total = total + rs[src]
    outer = contract_rows(total, total)[WIDTH:] * (1.0 / LEN)
    lanes = lax.broadcasted_iota(jnp.int32, (WIDTH, 2 * WIDTH), 1)
    squares = jnp.sum(outer * outer, axis=0, keepdims=True)
    squares = pltpu.roll(jnp.broadcast_to(squares, (8, 2 * WIDTH)), WIDTH, 1)
    squares = jnp.broadcast_to(squares[0:1], (WIDTH, 2 * WIDTH))
    mpad[...] = jnp.where(lanes < WIDTH, outer, squares)

    def rows8(i):
        return pl.ds(pl.multiple_of(i * 8, 8), 8)

    for d in range(1, NT):
        to = at_t(d)
        send(
            mpad.at[rows8(to)], a2a.at[rows8(t)], a2a_s.at[d], a2a_r.at[t], r, to
        )
    for d in range(1, NY):
        to = at_y(d)
        send(
            mpad.at[rows8(to)], ly.at[rows8(y)], ly_s.at[d], ly_r.at[y], to * NZ + z, t
        )
    a2a[rows8(t), :] = mpad[rows8(t), :]
    ly[rows8(y), :] = mpad[rows8(y), :]

    for d in range(1, NT):
        src = at_t(d)
        remote(
            a2a.at[rows8(src)], a2a.at[rows8(src)], a2a_s.at[d], a2a_r.at[src], r, src
        ).wait_recv()
    lane8 = lax.broadcasted_iota(jnp.int32, (8, 2 * WIDTH), 1)
    sub8 = lax.broadcasted_iota(jnp.int32, (8, 2 * WIDTH), 0)
    for k in range(4):
        even = a2a[pl.ds(2 * k, 8, stride=8), :]
        odd = a2a[pl.ds(2 * k + 1, 8, stride=8), :]
        tile = jnp.where(lane8 < WIDTH, even, pltpu.roll(odd, WIDTH, 1))
        v_lu[:, k * 128 : (k + 1) * 128] = tile[0:4]
        v_ld[:, k * 128 : (k + 1) * 128] = tile[4:8]
        half = ra if k < 2 else rb
        half[z, y, :, (k % 2) * 128 : (k % 2 + 1) * 128] = tile

    for d in range(1, NZ):
        to = at_z(d)
        send(
            ra.at[z, y], ra.at[z, y], p1a_s.at[d], p1a_r.at[z], y * NZ + to, t
        )
        to = at_y(d)
        send(
            rb.at[z, y], rb.at[z, y], p1b_s.at[d], p1b_r.at[y], to * NZ + z, t
        )

    write(v_lu, log_up)
    write(v_ld, log_dn)

    for d in range(1, NY):
        src = at_y(d)
        remote(
            ly.at[rows8(src)], ly.at[rows8(src)], ly_s.at[d], ly_r.at[src], src * NZ + z, t
        ).wait_recv()
    for i in range(NZ):
        lz[i] = ly[pl.ds(i, 8, stride=8), :]
    for d in range(1, NZ):
        to = at_z(d)
        slot = pl.ds(pl.multiple_of(t * 64 + z * 8, 8), 8)
        send(lz.at[to], lbuf.at[slot], lz_s.at[d], lz_r.at[z], y * NZ + to, t)
    lbuf[pl.ds(pl.multiple_of(t * 64 + z * 8, 8), 8), :] = lz[z]

    def block(h, c, k):
        if h == 0:
            return ra.at[pl.ds(2 * c, 2), at_y(k + NY)]
        return rb.at[at_z(k + NZ), pl.ds(2 * c, 2)]

    def pass_on(h, c, k, shift, kind):
        ref = block(h, c, k)
        dp = at_y(shift + NY) * NZ + z if h == 0 else y * NZ + at_z(shift + NZ)
        seen = k - shift if k - shift > -4 else 4
        base = (h * 4 + c) * 8
        send(ref, ref, p2_s.at[base + kind], p2_r.at[base + seen + 3], dp, t)

    def arrived(h, c, k):
        ref = block(h, c, k)
        index = (h * 4 + c) * 8 + k + 3
        remote(ref, ref, p2_s.at[index], p2_r.at[index], r, t).wait_recv()

    for c in range(4):
        for h in range(2):
            for s in (2 * c, 2 * c + 1):

                @pl.when((z if h == 0 else y) != s)
                def _():
                    ref = ra.at[s, y] if h == 0 else rb.at[z, s]
                    sem = p1a_r if h == 0 else p1b_r
                    remote(ref, ref, p1a_s.at[0], sem.at[s], r, t).wait_recv()

            for kind, shift in enumerate((2, -2, 1, -1)):
                pass_on(h, c, 0, shift, kind)

    for d in range(1, NZ):
        src = at_z(d)
        slot = pl.ds(pl.multiple_of(t * 64 + src * 8, 8), 8)
        remote(lbuf.at[slot], lbuf.at[slot], lz_s.at[d], lz_r.at[src], r, t).wait_recv()

    def rows64(i):
        return pl.ds(pl.multiple_of(i * 64, 64), 64)

    for d in range(1, NT):
        send(lbuf.at[rows64(t)], lbuf.at[rows64(t)], lt_s.at[d], lt_r.at[t], r, at_t(d))

    for c in range(4):
        for h in range(2):
            arrived(h, c, -2)
            if c % 2 == 0:
                pass_on(h, c, -2, 2, 6)
            pass_on(h, c, -2, 1, 4)
            arrived(h, c, 2)
            if c % 2 == 1:
                pass_on(h, c, 2, -2, 6)
            pass_on(h, c, 2, -1, 5)

    for d in range(1, NT):
        src = at_t(d)
        remote(
            lbuf.at[rows64(src)], lbuf.at[rows64(src)], lt_s.at[d], lt_r.at[src], r, t
        ).wait_recv()
    tally = jnp.zeros((8, 2 * WIDTH), jnp.float32)
    for i in range(NY * NZ):
        tile = lbuf[pl.ds(i, 8, stride=64), :]
        tally = tally + tile
        low = jnp.where((sub8 < 4) & (lane8 < WIDTH), tile, 0.0)
        high = jnp.where((sub8 >= 4) & (lane8 >= WIDTH), pltpu.roll(tile, WIDTH, 1), 0.0)
        lp[i * 8 : (i + 1) * 8, :] = low + high
    tally = jnp.where(lane8 >= WIDTH, tally, 0.0)
    trace_up = jnp.sum(jnp.where(sub8 < 4, tally, 0.0)) / SEQS
    trace_dn = jnp.sum(jnp.where(sub8 >= 4, tally, 0.0)) / SEQS

    row_ids = r * WIDTH + lax.broadcasted_iota(jnp.int32, (WIDTH, HALF), 0)
    col_ids = t * COLS + lax.broadcasted_iota(jnp.int32, (WIDTH, HALF), 1)
    for h in range(2):
        for c in range(4):
            for k in (-1, 1, -3, 3, 4):
                arrived(h, c, k)
        half = ra if h == 0 else rb
        gram = contract_rows(lp[...], half[...].reshape(8 * NY * NZ, HALF)) * (1.0 / SEQS)
        same = row_ids == col_ids + h * HALF
        cut = slice(h * HALF, (h + 1) * HALF)
        v_fu[:, cut] = gram[:WIDTH] + jnp.where(same, DAMPING * trace_up / FLAT, 0.0)
        v_fd[:, cut] = gram[WIDTH:] + jnp.where(same, DAMPING * trace_dn / FLAT, 0.0)
        write(v_fu.at[:, cut], f_up.at[:, cut])
        write(v_fd.at[:, cut], f_dn.at[:, cut])

    finish()
    for copy in writes:
        copy.wait()


def hand_over(*refs):
    given, taken, held = refs[0:4], refs[4:8], refs[8:12]
    sem_in, sem_out = refs[12:]
    order = (2, 3, 0, 1)
    ins = [pltpu.make_async_copy(given[i], held[i], sem_in.at[i]) for i in order]
    outs = [pltpu.make_async_copy(held[i], taken[i], sem_out.at[i]) for i in order]
    for copy in ins:
        copy.start()
    for copy, onward in zip(ins, outs, strict=True):
        copy.wait()
        onward.start()
    for onward in outs:
        onward.wait()


def body(
    input_acts, hidden_acts, up_grads, output_grads, inner_up, outer_up, inner_down, outer_down
):
    operands = (
        input_acts,
        hidden_acts,
        up_grads,
        output_grads,
        inner_up,
        outer_up,
        inner_down,
        outer_down,
    )
    f32 = jnp.float32
    dma = pltpu.SemaphoreType.DMA
    shapes = [(NT // 2, COLS)] * 2 + [(WIDTH, COLS)] * 2
    out_shape = [jax.ShapeDtypeStruct(shape, f32) for shape in shapes]
    results = pl.pallas_call(
        kernel,
        out_shape=out_shape,
        in_specs=[pl.BlockSpec(memory_space=pltpu.HBM)] * 8,
        out_specs=[pl.BlockSpec(memory_space=pltpu.HBM)] * 4,
        scratch_shapes=[pltpu.VMEM(a.shape, a.dtype) for a in operands]
        + [
            pltpu.VMEM((NT, LEN, 2 * WIDTH), f32),
            pltpu.VMEM((NT, LEN, 2 * WIDTH), f32),
            pltpu.VMEM((WIDTH, 2 * WIDTH), f32),
            pltpu.VMEM((8 * NT, 2 * WIDTH), f32),
            pltpu.VMEM((8 * NY, 2 * WIDTH), f32),
            pltpu.VMEM((NZ, NY, 2 * WIDTH), f32),
            pltpu.VMEM((NT * NZ * NY, 2 * WIDTH), f32),
            pltpu.VMEM((NT * NZ * NY, 2 * WIDTH), f32),
            pltpu.VMEM((NZ, NY, 8, HALF), f32),
            pltpu.VMEM((NZ, NY, 8, HALF), f32),
        ]
        + [pltpu.VMEM(shape, f32) for shape in shapes]
        + [dma((6 + 2 * LOADS,)), dma((6,))]
        + [dma((8,))] * 14
        + [dma((64,))] * 2,
        compiler_params=pltpu.CompilerParams(
            collective_id=0, has_side_effects=True, vmem_limit_bytes=63 * 1024 * 1024
        ),
        cost_estimate=pl.CostEstimate(
            flops=2 * 256 * 64 * 9216, bytes_accessed=6 * 1024 * 1024, transcendentals=0
        ),
    )(*operands)
    return pl.pallas_call(
        hand_over,
        out_shape=out_shape,
        in_specs=[pl.BlockSpec(memory_space=pltpu.HBM)] * 4,
        out_specs=[pl.BlockSpec(memory_space=pltpu.HBM)] * 4,
        scratch_shapes=[pltpu.VMEM(shape, f32) for shape in shapes] + [dma((4,))] * 2,
    )(*results)


def solution(mesh):
    split = P("dp", "tensor")
    basis = P(None, "tensor")
    return jax.shard_map(
        body,
        mesh=mesh,
        in_specs=(split,) * 4 + (basis,) * 4,
        out_specs=(split,) * 4,
        check_vma=False,
    )
```

```python
import jax
import jax.numpy as jnp
from jax import lax
from jax.experimental import pallas as pl
from jax.experimental.pallas import tpu as pltpu
from jax.sharding import PartitionSpec as P

LEN = 64
DAMPING = 0.5
WIDTH = 64
NT = 8
NY = 8
NZ = 8
SEQS = 256
FLAT = WIDTH * WIDTH
COLS = FLAT // NT
HALF = COLS // 2
PIECES = 4
SLOTS = 8 // PIECES
CUTS = (0, 512, 1536, 3584)
FAR_FIRST = (4, 3, 5, 2, 6, 1, 7)
MESH = pl.DeviceIdType.MESH


def project(acts, basis):
    return lax.dot_general(
        acts, basis, (((1,), (1,)), ((), ())), preferred_element_type=jnp.float32
    )


def split(values):
    high = values.astype(jnp.bfloat16)
    return high, (values - high.astype(jnp.float32)).astype(jnp.bfloat16)


def times(left, right):
    def dot(a, b):
        return lax.dot_general(
            a, b, (((1,), (0,)), ((), ())), preferred_element_type=jnp.float32
        )

    cross = dot(left[0], right[1]) + dot(left[1], right[0])
    return cross + dot(left[0], right[0])


def kernel(
    ia, ha, ug, og, iu, ou, idn, od,
    log_up, log_dn, f_up, f_dn,
    x_ia, x_ha, x_ug, x_og, w_iu, w_ou, w_id, w_od,
    part, rs, mpad, a2a, ly, lz, lbuf, lp, ra, rb,
    v_lu, v_ld, v_fu, v_fd,
    load_sem, out_sem,
    rs_s, rs_r, a2a_s, a2a_r, ly_s, ly_r, lz_s, lz_r, lt_s, lt_r,
    p1a_s, p1a_r, p1b_s, p1b_r, p2_s, p2_r,
):
    t = lax.axis_index("tensor")
    r = lax.axis_index("dp")
    y = r // NZ
    z = r % NZ

    def at_t(d):
        return (t + d) % NT

    x = t // 2

    def item_of(device):
        return device % 2 * (NT // 2) + device // 2

    item = item_of(t)

    def at_y(d):
        return (y + d) % NY

    def at_z(d):
        return (z + d) % NZ

    def remote(src, dst, send, recv, dp, tensor):
        return pltpu.make_async_remote_copy(
            src_ref=src,
            dst_ref=dst,
            send_sem=send,
            recv_sem=recv,
            device_id=(dp, tensor),
            device_id_type=MESH,
        )

    started = []

    def send(*copy_of):
        copy = remote(*copy_of)
        copy.start()
        started.append(copy)

    writes = []

    def write(src, dst):
        copy = pltpu.make_async_copy(src, dst, out_sem.at[len(writes)])
        copy.start()
        writes.append(copy)

    def settle():
        for copy in started:
            copy.wait_send()
        started.clear()

    barrier = pltpu.get_barrier_semaphore()
    for d in range(1, NT):
        pl.semaphore_signal(barrier, inc=1, device_id=(r, at_t(d)), device_id_type=MESH)
    for d in range(1, NY):
        pl.semaphore_signal(barrier, inc=1, device_id=(at_y(d) * NZ + z, t), device_id_type=MESH)
    for d in range(1, NZ):
        pl.semaphore_signal(barrier, inc=1, device_id=(y * NZ + at_z(d), t), device_id_type=MESH)

    loads = []

    def load(src, dst):
        copy = pltpu.make_async_copy(src, dst, load_sem.at[len(loads)])
        copy.start()
        loads.append(copy)
        return copy

    def wide_loads(src, dst):
        return [
            load(src.at[:, pl.ds(a, b - a)], dst.at[:, pl.ds(a, b - a)])
            for a, b in zip(CUTS[:-1], CUTS[1:], strict=True)
        ]

    up_narrow = [load(iu, w_iu), load(ia, x_ia)]
    up_basis = load(ou, w_ou)
    up_wide = wide_loads(ug, x_ug)
    dn_narrow = [load(od, w_od), load(og, x_og)]
    dn_basis = load(idn, w_id)
    dn_wide = wide_loads(ha, x_ha)

    def projected(narrow, basis, wides, x_n, w_n, x_w, w_w):
        for copy in narrow:
            copy.wait()
        slim = project(x_n[...], w_n[...])
        basis.wait()
        total = None
        for c, copy in enumerate(wides):
            copy.wait()
            cut = slice(CUTS[c], CUTS[c + 1])
            term = project(x_w[:, cut], w_w[:, cut])
            total = term if total is None else total + term
        return slim, total

    def scatter(side):
        for d in range(NT // 2):
            other = (x + d) % (NT // 2)
            m = side * (NT // 2) + other
            to = 2 * other + side

            @pl.when(t != to)
            def _():
                remote(part.at[m], rs.at[t], rs_s.at[m], rs_r.at[t], r, to).start()

    act, grad = projected(up_narrow, up_basis, up_wide, x_ia, w_iu, x_ug, w_ou)
    part[0 : NT // 2] = jnp.concatenate([act, grad], axis=1).reshape(NT // 2, LEN, 2 * WIDTH)
    pl.semaphore_wait(barrier, (NT - 1) + (NY - 1) + (NZ - 1))
    scatter(0)
    grad, act = projected(dn_narrow, dn_basis, dn_wide, x_og, w_od, x_ha, w_id)
    part[NT // 2 :] = jnp.concatenate([act, grad], axis=1).reshape(NT // 2, LEN, 2 * WIDTH)
    scatter(1)

    total = part[item]
    for d in range(1, NT):
        src = at_t(d)
        remote(rs.at[src], rs.at[src], rs_s.at[src], rs_r.at[src], r, src).wait_recv()
        total = total + rs[src]
    outer = times(split(total.T), split(total))[WIDTH:] * (1.0 / LEN)
    lanes = lax.broadcasted_iota(jnp.int32, (WIDTH, 2 * WIDTH), 1)
    squares = jnp.sum(outer * outer, axis=0, keepdims=True)
    squares = pltpu.roll(jnp.broadcast_to(squares, (8, 2 * WIDTH)), WIDTH, 1)
    squares = jnp.broadcast_to(squares[0:1], (WIDTH, 2 * WIDTH))
    mpad[...] = jnp.where(lanes < WIDTH, outer, squares)

    def rows8(i):
        return pl.ds(pl.multiple_of(i * 8, 8), 8)

    for d in FAR_FIRST:
        to = at_t(d)
        send(
            mpad.at[rows8(to)], a2a.at[rows8(item)], a2a_s.at[d], a2a_r.at[t], r, to
        )
    for d in FAR_FIRST:
        to = at_y(d)
        send(
            mpad.at[rows8(to)], ly.at[rows8(y)], ly_s.at[d], ly_r.at[y], to * NZ + z, t
        )
    a2a[rows8(item), :] = mpad[rows8(t), :]
    ly[rows8(y), :] = mpad[rows8(y), :]

    for d in range(1, NT):
        src = at_t(d)
        remote(
            a2a.at[rows8(item_of(src))], a2a.at[rows8(item_of(src))], a2a_s.at[d], a2a_r.at[src], r, src
        ).wait_recv()
    lane8 = lax.broadcasted_iota(jnp.int32, (8, 2 * WIDTH), 1)
    sub8 = lax.broadcasted_iota(jnp.int32, (8, 2 * WIDTH), 0)
    for k in range(4):
        even = a2a[pl.ds(2 * k, 8, stride=8), :]
        odd = a2a[pl.ds(2 * k + 1, 8, stride=8), :]
        tile = jnp.where(lane8 < WIDTH, even, pltpu.roll(odd, WIDTH, 1))
        v_lu[:, k * 128 : (k + 1) * 128] = tile[0:4]
        v_ld[:, k * 128 : (k + 1) * 128] = tile[4:8]
        half = ra if k < 2 else rb
        half[z, y, :, (k % 2) * 128 : (k % 2 + 1) * 128] = tile

    for d in FAR_FIRST:
        to = at_z(d)
        send(
            ra.at[z, y], ra.at[z, y], p1a_s.at[d], p1a_r.at[z], y * NZ + to, t
        )
        to = at_y(d)
        send(
            rb.at[z, y], rb.at[z, y], p1b_s.at[d], p1b_r.at[y], to * NZ + z, t
        )

    write(v_lu, log_up)
    write(v_ld, log_dn)

    for d in range(1, NY):
        src = at_y(d)
        remote(
            ly.at[rows8(src)], ly.at[rows8(src)], ly_s.at[d], ly_r.at[src], src * NZ + z, t
        ).wait_recv()
    for i in range(NZ):
        lz[i] = ly[pl.ds(i, 8, stride=8), :]
    for d in FAR_FIRST:
        to = at_z(d)
        slot = pl.ds(pl.multiple_of(item * 64 + z * 8, 8), 8)
        send(lz.at[to], lbuf.at[slot], lz_s.at[d], lz_r.at[z], y * NZ + to, t)
    lbuf[pl.ds(pl.multiple_of(item * 64 + z * 8, 8), 8), :] = lz[z]

    def block(h, c, k):
        if h == 0:
            return ra.at[pl.ds(SLOTS * c, SLOTS), at_y(k + NY)]
        return rb.at[at_z(k + NZ), pl.ds(SLOTS * c, SLOTS)]

    def pass_on(h, c, k, shift, kind):
        ref = block(h, c, k)
        dp = at_y(shift + NY) * NZ + z if h == 0 else y * NZ + at_z(shift + NZ)
        seen = k - shift if k - shift > -4 else 4
        base = (h * PIECES + c) * 8
        send(ref, ref, p2_s.at[base + kind], p2_r.at[base + seen + 3], dp, t)

    def arrived(h, c, k):
        ref = block(h, c, k)
        index = (h * PIECES + c) * 8 + k + 3
        remote(ref, ref, p2_s.at[index], p2_r.at[index], r, t).wait_recv()

    for c in range(PIECES):
        for h in range(2):
            for s in range(SLOTS * c, SLOTS * (c + 1)):

                @pl.when((z if h == 0 else y) != s)
                def _():
                    ref = ra.at[s, y] if h == 0 else rb.at[z, s]
                    sem = p1a_r if h == 0 else p1b_r
                    remote(ref, ref, p1a_s.at[0], sem.at[s], r, t).wait_recv()

            for kind, shift in enumerate((2, -2, 1, -1)):
                pass_on(h, c, 0, shift, kind)

    for d in range(1, NZ):
        src = at_z(d)
        slot = pl.ds(pl.multiple_of(item * 64 + src * 8, 8), 8)
        remote(lbuf.at[slot], lbuf.at[slot], lz_s.at[d], lz_r.at[src], r, t).wait_recv()

    def rows64(i):
        return pl.ds(pl.multiple_of(i * 64, 64), 64)

    for d in range(1, NT):
        send(lbuf.at[rows64(item)], lbuf.at[rows64(item)], lt_s.at[d], lt_r.at[t], r, at_t(d))

    for c in range(PIECES):
        for h in range(2):
            arrived(h, c, -2)
            if c % 2 == 0:
                pass_on(h, c, -2, 2, 6)
            pass_on(h, c, -2, 1, 4)
            arrived(h, c, 2)
            if c % 2 == 1:
                pass_on(h, c, 2, -2, 6)
            pass_on(h, c, 2, -1, 5)

    for m in range(NT):

        @pl.when(item != m)
        def _():
            remote(part.at[m], rs.at[t], rs_s.at[m], rs_r.at[t], r, m).wait_send()

    settle()
    for d in range(1, NT):
        src = at_t(d)
        remote(
            lbuf.at[rows64(item_of(src))], lbuf.at[rows64(item_of(src))], lt_s.at[d], lt_r.at[src], r, t
        ).wait_recv()
    tally = jnp.zeros((8, 2 * WIDTH), jnp.float32)
    for i in range(NY * NZ):
        tile = lbuf[pl.ds(i, 8, stride=64), :]
        tally = tally + tile
        low = jnp.where((sub8 < 4) & (lane8 < WIDTH), tile, 0.0)
        high = jnp.where((sub8 >= 4) & (lane8 >= WIDTH), pltpu.roll(tile, WIDTH, 1), 0.0)
        lp[i * 8 : (i + 1) * 8, :] = low + high
    tally = jnp.where(lane8 >= WIDTH, tally, 0.0)
    trace_up = jnp.sum(jnp.where(sub8 < 4, tally, 0.0)) / SEQS
    trace_dn = jnp.sum(jnp.where(sub8 >= 4, tally, 0.0)) / SEQS

    left = split(lp[...].T)
    row_ids = r * WIDTH + lax.broadcasted_iota(jnp.int32, (WIDTH, HALF), 0)
    col_ids = t * COLS + lax.broadcasted_iota(jnp.int32, (WIDTH, HALF), 1)
    for h in range(2):
        for c in range(PIECES):
            for k in (-1, 1, -3, 3, 4):
                arrived(h, c, k)
        half = ra if h == 0 else rb
        gram = times(left, split(half[...].reshape(8 * NY * NZ, HALF))) * (1.0 / SEQS)
        same = row_ids == col_ids + h * HALF
        cut = slice(h * HALF, (h + 1) * HALF)
        v_fu[:, cut] = gram[:WIDTH] + jnp.where(same, DAMPING * trace_up / FLAT, 0.0)
        v_fd[:, cut] = gram[WIDTH:] + jnp.where(same, DAMPING * trace_dn / FLAT, 0.0)
        write(v_fu.at[:, cut], f_up.at[:, cut])
        write(v_fd.at[:, cut], f_dn.at[:, cut])

    settle()
    for copy in writes:
        copy.wait()


def hand_over(*refs):
    given, taken, held = refs[0:4], refs[4:8], refs[8:12]
    sem_in, sem_out = refs[12:]
    order = (2, 3, 0, 1)
    ins = [pltpu.make_async_copy(given[i], held[i], sem_in.at[i]) for i in order]
    outs = [pltpu.make_async_copy(held[i], taken[i], sem_out.at[i]) for i in order]
    for copy in ins:
        copy.start()
    for copy, onward in zip(ins, outs, strict=True):
        copy.wait()
        onward.start()
    for onward in outs:
        onward.wait()


def body(
    input_acts, hidden_acts, up_grads, output_grads, inner_up, outer_up, inner_down, outer_down
):
    operands = (
        input_acts,
        hidden_acts,
        up_grads,
        output_grads,
        inner_up,
        outer_up,
        inner_down,
        outer_down,
    )
    f32 = jnp.float32
    dma = pltpu.SemaphoreType.DMA
    shapes = [(NT // 2, COLS)] * 2 + [(WIDTH, COLS)] * 2
    out_shape = [jax.ShapeDtypeStruct(shape, f32) for shape in shapes]
    results = pl.pallas_call(
        kernel,
        out_shape=out_shape,
        in_specs=[pl.BlockSpec(memory_space=pltpu.HBM)] * 8,
        out_specs=[pl.BlockSpec(memory_space=pltpu.HBM)] * 4,
        scratch_shapes=[pltpu.VMEM(a.shape, a.dtype) for a in operands]
        + [
            pltpu.VMEM((NT, LEN, 2 * WIDTH), f32),
            pltpu.VMEM((NT, LEN, 2 * WIDTH), f32),
            pltpu.VMEM((WIDTH, 2 * WIDTH), f32),
            pltpu.VMEM((8 * NT, 2 * WIDTH), f32),
            pltpu.VMEM((8 * NY, 2 * WIDTH), f32),
            pltpu.VMEM((NZ, NY, 2 * WIDTH), f32),
            pltpu.VMEM((NT * NZ * NY, 2 * WIDTH), f32),
            pltpu.VMEM((NT * NZ * NY, 2 * WIDTH), f32),
            pltpu.VMEM((NZ, NY, 8, HALF), f32),
            pltpu.VMEM((NZ, NY, 8, HALF), f32),
        ]
        + [pltpu.VMEM(shape, f32) for shape in shapes]
        + [dma((6 + 2 * (len(CUTS) - 1),)), dma((6,))]
        + [dma((8,))] * 14
        + [dma((64,))] * 2,
        compiler_params=pltpu.CompilerParams(
            collective_id=0, has_side_effects=True, vmem_limit_bytes=63 * 1024 * 1024
        ),
        cost_estimate=pl.CostEstimate(
            flops=2 * 256 * 64 * 9216, bytes_accessed=6 * 1024 * 1024, transcendentals=0
        ),
    )(*operands)
    return pl.pallas_call(
        hand_over,
        out_shape=out_shape,
        in_specs=[pl.BlockSpec(memory_space=pltpu.HBM)] * 4,
        out_specs=[pl.BlockSpec(memory_space=pltpu.HBM)] * 4,
        scratch_shapes=[pltpu.VMEM(shape, f32) for shape in shapes] + [dma((4,))] * 2,
    )(*results)


def solution(mesh):
    split = P("dp", "tensor")
    basis = P(None, "tensor")
    return jax.shard_map(
        body,
        mesh=mesh,
        in_specs=(split,) * 4 + (basis,) * 4,
        out_specs=(split,) * 4,
        check_vma=False,
    )
```

```python
import jax
import jax.numpy as jnp
from jax import lax
from jax.experimental import pallas as pl
from jax.experimental.pallas import tpu as pltpu
from jax.sharding import PartitionSpec as P

LEN = 64
DAMPING = 0.5
WIDTH = 64
NT = 8
NY = 8
NZ = 8
SEQS = 256
FLAT = WIDTH * WIDTH
COLS = FLAT // NT
HALF = COLS // 2
PIECES = 4
SLOTS = 8 // PIECES
CUTS = (0, 512, 1536, 3584)
FAR_FIRST = (4, 3, 5, 2, 6, 1, 7)
MESH = pl.DeviceIdType.MESH


def project(acts, basis):
    return lax.dot_general(
        acts, basis, (((1,), (1,)), ((), ())), preferred_element_type=jnp.float32
    )


def split(values):
    high = values.astype(jnp.bfloat16)
    return high, (values - high.astype(jnp.float32)).astype(jnp.bfloat16)


def times(left, right):
    def dot(a, b):
        return lax.dot_general(
            a, b, (((1,), (0,)), ((), ())), preferred_element_type=jnp.float32
        )

    cross = dot(left[0], right[1]) + dot(left[1], right[0])
    return cross + dot(left[0], right[0])


def kernel(
    ia, ha, ug, og, iu, ou, idn, od,
    v_lu, v_ld, v_fu, v_fd,
    x_ia, x_ha, x_ug, x_og, w_iu, w_ou, w_id, w_od,
    part, rs, mpad, a2a, ly, lz, lbuf, lp, ra, rb,
    load_sem,
    rs_s, rs_r, a2a_s, a2a_r, ly_s, ly_r, lz_s, lz_r, lt_s, lt_r,
    p1a_s, p1a_r, p1b_s, p1b_r, p2_s, p2_r,
):
    t = lax.axis_index("tensor")
    r = lax.axis_index("dp")
    y = r // NZ
    z = r % NZ

    def at_t(d):
        return (t + d) % NT

    x = t // 2

    def item_of(device):
        return device % 2 * (NT // 2) + device // 2

    item = item_of(t)

    def at_y(d):
        return (y + d) % NY

    def at_z(d):
        return (z + d) % NZ

    def remote(src, dst, send, recv, dp, tensor):
        return pltpu.make_async_remote_copy(
            src_ref=src,
            dst_ref=dst,
            send_sem=send,
            recv_sem=recv,
            device_id=(dp, tensor),
            device_id_type=MESH,
        )

    started = []

    def send(*copy_of):
        copy = remote(*copy_of)
        copy.start()
        started.append(copy)

    def settle():
        for copy in started:
            copy.wait_send()
        started.clear()

    barrier = pltpu.get_barrier_semaphore()
    for d in range(1, NT):
        pl.semaphore_signal(barrier, inc=1, device_id=(r, at_t(d)), device_id_type=MESH)
    for d in range(1, NY):
        pl.semaphore_signal(barrier, inc=1, device_id=(at_y(d) * NZ + z, t), device_id_type=MESH)
    for d in range(1, NZ):
        pl.semaphore_signal(barrier, inc=1, device_id=(y * NZ + at_z(d), t), device_id_type=MESH)

    loads = []

    def load(src, dst):
        copy = pltpu.make_async_copy(src, dst, load_sem.at[len(loads)])
        copy.start()
        loads.append(copy)
        return copy

    def wide_loads(src, dst):
        return [
            load(src.at[:, pl.ds(a, b - a)], dst.at[:, pl.ds(a, b - a)])
            for a, b in zip(CUTS[:-1], CUTS[1:], strict=True)
        ]

    up_narrow = [load(iu, w_iu), load(ia, x_ia)]
    up_basis = load(ou, w_ou)
    up_wide = wide_loads(ug, x_ug)
    dn_narrow = [load(od, w_od), load(og, x_og)]
    dn_basis = load(idn, w_id)
    dn_wide = wide_loads(ha, x_ha)

    def projected(narrow, basis, wides, x_n, w_n, x_w, w_w):
        for copy in narrow:
            copy.wait()
        slim = project(x_n[...], w_n[...])
        basis.wait()
        total = None
        for c, copy in enumerate(wides):
            copy.wait()
            cut = slice(CUTS[c], CUTS[c + 1])
            term = project(x_w[:, cut], w_w[:, cut])
            total = term if total is None else total + term
        return slim, total

    def scatter(side):
        for d in range(NT // 2):
            other = (x + d) % (NT // 2)
            m = side * (NT // 2) + other
            to = 2 * other + side

            @pl.when(t != to)
            def _():
                remote(part.at[m], rs.at[t], rs_s.at[m], rs_r.at[t], r, to).start()

    act, grad = projected(up_narrow, up_basis, up_wide, x_ia, w_iu, x_ug, w_ou)
    part[0 : NT // 2] = jnp.concatenate([act, grad], axis=1).reshape(NT // 2, LEN, 2 * WIDTH)
    pl.semaphore_wait(barrier, (NT - 1) + (NY - 1) + (NZ - 1))
    scatter(0)
    grad, act = projected(dn_narrow, dn_basis, dn_wide, x_og, w_od, x_ha, w_id)
    part[NT // 2 :] = jnp.concatenate([act, grad], axis=1).reshape(NT // 2, LEN, 2 * WIDTH)
    scatter(1)

    total = part[item]
    for d in range(1, NT):
        src = at_t(d)
        remote(rs.at[src], rs.at[src], rs_s.at[src], rs_r.at[src], r, src).wait_recv()
        total = total + rs[src]
    outer = times(split(total.T), split(total))[WIDTH:] * (1.0 / LEN)
    lanes = lax.broadcasted_iota(jnp.int32, (WIDTH, 2 * WIDTH), 1)
    squares = jnp.sum(outer * outer, axis=0, keepdims=True)
    squares = pltpu.roll(jnp.broadcast_to(squares, (8, 2 * WIDTH)), WIDTH, 1)
    squares = jnp.broadcast_to(squares[0:1], (WIDTH, 2 * WIDTH))
    mpad[...] = jnp.where(lanes < WIDTH, outer, squares)

    def rows8(i):
        return pl.ds(pl.multiple_of(i * 8, 8), 8)

    for d in FAR_FIRST:
        to = at_t(d)
        send(
            mpad.at[rows8(to)], a2a.at[rows8(item)], a2a_s.at[d], a2a_r.at[t], r, to
        )
    for d in FAR_FIRST:
        to = at_y(d)
        send(
            mpad.at[rows8(to)], ly.at[rows8(y)], ly_s.at[d], ly_r.at[y], to * NZ + z, t
        )
    a2a[rows8(item), :] = mpad[rows8(t), :]
    ly[rows8(y), :] = mpad[rows8(y), :]

    for d in range(1, NT):
        src = at_t(d)
        remote(
            a2a.at[rows8(item_of(src))], a2a.at[rows8(item_of(src))], a2a_s.at[d], a2a_r.at[src], r, src
        ).wait_recv()
    lane8 = lax.broadcasted_iota(jnp.int32, (8, 2 * WIDTH), 1)
    sub8 = lax.broadcasted_iota(jnp.int32, (8, 2 * WIDTH), 0)
    for k in range(4):
        even = a2a[pl.ds(2 * k, 8, stride=8), :]
        odd = a2a[pl.ds(2 * k + 1, 8, stride=8), :]
        tile = jnp.where(lane8 < WIDTH, even, pltpu.roll(odd, WIDTH, 1))
        v_lu[:, k * 128 : (k + 1) * 128] = tile[0:4]
        v_ld[:, k * 128 : (k + 1) * 128] = tile[4:8]
        half = ra if k < 2 else rb
        half[z, y, :, (k % 2) * 128 : (k % 2 + 1) * 128] = tile

    for d in FAR_FIRST:
        to = at_z(d)
        send(
            ra.at[z, y], ra.at[z, y], p1a_s.at[d], p1a_r.at[z], y * NZ + to, t
        )
        to = at_y(d)
        send(
            rb.at[z, y], rb.at[z, y], p1b_s.at[d], p1b_r.at[y], to * NZ + z, t
        )


    for d in range(1, NY):
        src = at_y(d)
        remote(
            ly.at[rows8(src)], ly.at[rows8(src)], ly_s.at[d], ly_r.at[src], src * NZ + z, t
        ).wait_recv()
    for i in range(NZ):
        lz[i] = ly[pl.ds(i, 8, stride=8), :]
    for d in FAR_FIRST:
        to = at_z(d)
        slot = pl.ds(pl.multiple_of(item * 64 + z * 8, 8), 8)
        send(lz.at[to], lbuf.at[slot], lz_s.at[d], lz_r.at[z], y * NZ + to, t)
    lbuf[pl.ds(pl.multiple_of(item * 64 + z * 8, 8), 8), :] = lz[z]

    def block(h, c, k):
        if h == 0:
            return ra.at[pl.ds(SLOTS * c, SLOTS), at_y(k + NY)]
        return rb.at[at_z(k + NZ), pl.ds(SLOTS * c, SLOTS)]

    def pass_on(h, c, k, shift, kind):
        ref = block(h, c, k)
        dp = at_y(shift + NY) * NZ + z if h == 0 else y * NZ + at_z(shift + NZ)
        seen = k - shift if k - shift > -4 else 4
        base = (h * PIECES + c) * 8
        send(ref, ref, p2_s.at[base + kind], p2_r.at[base + seen + 3], dp, t)

    def arrived(h, c, k):
        ref = block(h, c, k)
        index = (h * PIECES + c) * 8 + k + 3
        remote(ref, ref, p2_s.at[index], p2_r.at[index], r, t).wait_recv()

    for c in range(PIECES):
        for h in range(2):
            for s in range(SLOTS * c, SLOTS * (c + 1)):

                @pl.when((z if h == 0 else y) != s)
                def _():
                    ref = ra.at[s, y] if h == 0 else rb.at[z, s]
                    sem = p1a_r if h == 0 else p1b_r
                    remote(ref, ref, p1a_s.at[0], sem.at[s], r, t).wait_recv()

            for kind, shift in enumerate((2, -2, 1, -1)):
                pass_on(h, c, 0, shift, kind)

    for d in range(1, NZ):
        src = at_z(d)
        slot = pl.ds(pl.multiple_of(item * 64 + src * 8, 8), 8)
        remote(lbuf.at[slot], lbuf.at[slot], lz_s.at[d], lz_r.at[src], r, t).wait_recv()

    def rows64(i):
        return pl.ds(pl.multiple_of(i * 64, 64), 64)

    for d in range(1, NT):
        send(lbuf.at[rows64(item)], lbuf.at[rows64(item)], lt_s.at[d], lt_r.at[t], r, at_t(d))

    for c in range(PIECES):
        for h in range(2):
            arrived(h, c, -2)
            if c % 2 == 0:
                pass_on(h, c, -2, 2, 6)
            pass_on(h, c, -2, 1, 4)
            arrived(h, c, 2)
            if c % 2 == 1:
                pass_on(h, c, 2, -2, 6)
            pass_on(h, c, 2, -1, 5)

    for m in range(NT):

        @pl.when(item != m)
        def _():
            remote(part.at[m], rs.at[t], rs_s.at[m], rs_r.at[t], r, m).wait_send()

    settle()
    for d in range(1, NT):
        src = at_t(d)
        remote(
            lbuf.at[rows64(item_of(src))], lbuf.at[rows64(item_of(src))], lt_s.at[d], lt_r.at[src], r, t
        ).wait_recv()
    tally = jnp.zeros((8, 2 * WIDTH), jnp.float32)
    for i in range(NY * NZ):
        tile = lbuf[pl.ds(i, 8, stride=64), :]
        tally = tally + tile
        low = jnp.where((sub8 < 4) & (lane8 < WIDTH), tile, 0.0)
        high = jnp.where((sub8 >= 4) & (lane8 >= WIDTH), pltpu.roll(tile, WIDTH, 1), 0.0)
        lp[i * 8 : (i + 1) * 8, :] = low + high
    tally = jnp.where(lane8 >= WIDTH, tally, 0.0)
    trace_up = jnp.sum(jnp.where(sub8 < 4, tally, 0.0)) / SEQS
    trace_dn = jnp.sum(jnp.where(sub8 >= 4, tally, 0.0)) / SEQS

    left = split(lp[...].T)
    row_ids = r * WIDTH + lax.broadcasted_iota(jnp.int32, (WIDTH, HALF), 0)
    col_ids = t * COLS + lax.broadcasted_iota(jnp.int32, (WIDTH, HALF), 1)
    for h in range(2):
        for c in range(PIECES):
            for k in (-1, 1, -3, 3, 4):
                arrived(h, c, k)
        half = ra if h == 0 else rb
        gram = times(left, split(half[...].reshape(8 * NY * NZ, HALF))) * (1.0 / SEQS)
        same = row_ids == col_ids + h * HALF
        cut = slice(h * HALF, (h + 1) * HALF)
        v_fu[:, cut] = gram[:WIDTH] + jnp.where(same, DAMPING * trace_up / FLAT, 0.0)
        v_fd[:, cut] = gram[WIDTH:] + jnp.where(same, DAMPING * trace_dn / FLAT, 0.0)

    settle()


def hand_over(*refs):
    given, taken, sems = refs[0:4], refs[4:8], refs[8]
    copies = [pltpu.make_async_copy(given[i], taken[i], sems.at[i]) for i in (2, 3, 0, 1)]
    for copy in copies:
        copy.start()
    for copy in copies:
        copy.wait()


def body(
    input_acts, hidden_acts, up_grads, output_grads, inner_up, outer_up, inner_down, outer_down
):
    operands = (
        input_acts,
        hidden_acts,
        up_grads,
        output_grads,
        inner_up,
        outer_up,
        inner_down,
        outer_down,
    )
    f32 = jnp.float32
    dma = pltpu.SemaphoreType.DMA
    shapes = [(NT // 2, COLS)] * 2 + [(WIDTH, COLS)] * 2
    out_shape = [jax.ShapeDtypeStruct(shape, f32) for shape in shapes]
    results = pl.pallas_call(
        kernel,
        out_shape=out_shape,
        in_specs=[pl.BlockSpec(memory_space=pltpu.HBM)] * 8,
        out_specs=[pl.BlockSpec(memory_space=pltpu.VMEM)] * 4,
        scratch_shapes=[pltpu.VMEM(a.shape, a.dtype) for a in operands]
        + [
            pltpu.VMEM((NT, LEN, 2 * WIDTH), f32),
            pltpu.VMEM((NT, LEN, 2 * WIDTH), f32),
            pltpu.VMEM((WIDTH, 2 * WIDTH), f32),
            pltpu.VMEM((8 * NT, 2 * WIDTH), f32),
            pltpu.VMEM((8 * NY, 2 * WIDTH), f32),
            pltpu.VMEM((NZ, NY, 2 * WIDTH), f32),
            pltpu.VMEM((NT * NZ * NY, 2 * WIDTH), f32),
            pltpu.VMEM((NT * NZ * NY, 2 * WIDTH), f32),
            pltpu.VMEM((NZ, NY, 8, HALF), f32),
            pltpu.VMEM((NZ, NY, 8, HALF), f32),
        ]
        + [dma((6 + 2 * (len(CUTS) - 1),))]
        + [dma((8,))] * 14
        + [dma((64,))] * 2,
        compiler_params=pltpu.CompilerParams(
            collective_id=0, has_side_effects=True, vmem_limit_bytes=54912 * 1024
        ),
        cost_estimate=pl.CostEstimate(
            flops=2 * 256 * 64 * 9216, bytes_accessed=6 * 1024 * 1024, transcendentals=0
        ),
    )(*operands)
    return pl.pallas_call(
        hand_over,
        out_shape=out_shape,
        in_specs=[pl.BlockSpec(memory_space=pltpu.VMEM)] * 4,
        out_specs=[pl.BlockSpec(memory_space=pltpu.HBM)] * 4,
        scratch_shapes=[dma((4,))],
        compiler_params=pltpu.CompilerParams(vmem_limit_bytes=1024 * 1024),
    )(*results)


def solution(mesh):
    split = P("dp", "tensor")
    basis = P(None, "tensor")
    return jax.shard_map(
        body,
        mesh=mesh,
        in_specs=(split,) * 4 + (basis,) * 4,
        out_specs=(split,) * 4,
        check_vma=False,
    )
```

```python
import jax
import jax.numpy as jnp
from jax import lax
from jax.experimental import pallas as pl
from jax.experimental.pallas import tpu as pltpu
from jax.sharding import PartitionSpec as P

LEN = 64
DAMPING = 0.5
WIDTH = 64
NT = 8
NY = 8
NZ = 8
SEQS = 256
FLAT = WIDTH * WIDTH
COLS = FLAT // NT
HALF = COLS // 2
PIECES = 4
SLOTS = 8 // PIECES
CUTS = (0, 512, 1536, 3584)
FAR_FIRST = (4, 3, 5, 2, 6, 1, 7)
MESH = pl.DeviceIdType.MESH


def project(acts, basis):
    return lax.dot_general(
        acts, basis, (((1,), (1,)), ((), ())), preferred_element_type=jnp.float32
    )


def split(values):
    high = values.astype(jnp.bfloat16)
    return high, (values - high.astype(jnp.float32)).astype(jnp.bfloat16)


def times(left, right):
    def dot(a, b):
        return lax.dot_general(
            a, b, (((1,), (0,)), ((), ())), preferred_element_type=jnp.float32
        )

    cross = dot(left[0], right[1]) + dot(left[1], right[0])
    return cross + dot(left[0], right[0])


def kernel(
    ia, ha, ug, og, iu, ou, idn, od,
    v_lu, v_ld, v_fu, v_fd,
    x_ia, x_ha, x_ug, x_og, w_iu, w_ou, w_id, w_od,
    part, rs, mpad, a2a, ly, lz, lbuf, lp, ra, rb,
    load_sem,
    rs_s, rs_r, a2a_s, a2a_r, ly_s, ly_r, lz_s, lz_r, lt_s, lt_r,
    p1a_s, p1a_r, p1b_s, p1b_r, p2_s, p2_r,
):
    t = lax.axis_index("tensor")
    r = lax.axis_index("dp")
    y = r // NZ
    z = r % NZ

    def at_t(d):
        return (t + d) % NT

    x = t // 2

    def item_of(device):
        return device % 2 * (NT // 2) + device // 2

    item = item_of(t)

    def at_y(d):
        return (y + d) % NY

    def at_z(d):
        return (z + d) % NZ

    def remote(src, dst, send, recv, dp, tensor):
        return pltpu.make_async_remote_copy(
            src_ref=src,
            dst_ref=dst,
            send_sem=send,
            recv_sem=recv,
            device_id=(dp, tensor),
            device_id_type=MESH,
        )

    started = []

    def send(*copy_of):
        copy = remote(*copy_of)
        copy.start()
        started.append(copy)

    def settle():
        for copy in started:
            copy.wait_send()
        started.clear()

    barrier = pltpu.get_barrier_semaphore()
    for d in range(1, NT):
        pl.semaphore_signal(barrier, inc=1, device_id=(r, at_t(d)), device_id_type=MESH)
    for d in range(1, NY):
        pl.semaphore_signal(barrier, inc=1, device_id=(at_y(d) * NZ + z, t), device_id_type=MESH)
    for d in range(1, NZ):
        pl.semaphore_signal(barrier, inc=1, device_id=(y * NZ + at_z(d), t), device_id_type=MESH)

    loads = []

    def load(src, dst):
        copy = pltpu.make_async_copy(src, dst, load_sem.at[len(loads)])
        copy.start()
        loads.append(copy)
        return copy

    def wide_loads(src, dst):
        return [
            load(src.at[:, pl.ds(a, b - a)], dst.at[:, pl.ds(a, b - a)])
            for a, b in zip(CUTS[:-1], CUTS[1:], strict=True)
        ]

    up_narrow = [load(iu, w_iu), load(ia, x_ia)]
    up_basis = load(ou, w_ou)
    up_wide = wide_loads(ug, x_ug)
    dn_narrow = [load(od, w_od), load(og, x_og)]
    dn_basis = load(idn, w_id)
    dn_wide = wide_loads(ha, x_ha)

    def projected(narrow, basis, wides, x_n, w_n, x_w, w_w):
        for copy in narrow:
            copy.wait()
        slim = project(x_n[...], w_n[...])
        basis.wait()
        total = None
        for c, copy in enumerate(wides):
            copy.wait()
            cut = slice(CUTS[c], CUTS[c + 1])
            term = project(x_w[:, cut], w_w[:, cut])
            total = term if total is None else total + term
        return slim, total

    def scatter(side):
        for d in (2, 1, 3, 0):
            other = (x + d) % (NT // 2)
            m = side * (NT // 2) + other
            to = 2 * other + side

            @pl.when(t != to)
            def _():
                remote(part.at[m], rs.at[t], rs_s.at[m], rs_r.at[t], r, to).start()

    act, grad = projected(up_narrow, up_basis, up_wide, x_ia, w_iu, x_ug, w_ou)
    part[0 : NT // 2] = jnp.concatenate([act, grad], axis=1).reshape(NT // 2, LEN, 2 * WIDTH)
    pl.semaphore_wait(barrier, (NT - 1) + (NY - 1) + (NZ - 1))
    scatter(0)
    grad, act = projected(dn_narrow, dn_basis, dn_wide, x_og, w_od, x_ha, w_id)
    part[NT // 2 :] = jnp.concatenate([act, grad], axis=1).reshape(NT // 2, LEN, 2 * WIDTH)
    scatter(1)

    total = part[item]
    for d in range(1, NT):
        src = at_t(d)
        remote(rs.at[src], rs.at[src], rs_s.at[src], rs_r.at[src], r, src).wait_recv()
        total = total + rs[src]
    outer = times(split(total.T), split(total))[WIDTH:] * (1.0 / LEN)
    lanes = lax.broadcasted_iota(jnp.int32, (WIDTH, 2 * WIDTH), 1)
    squares = jnp.sum(outer * outer, axis=0, keepdims=True)
    squares = pltpu.roll(jnp.broadcast_to(squares, (8, 2 * WIDTH)), WIDTH, 1)
    squares = jnp.broadcast_to(squares[0:1], (WIDTH, 2 * WIDTH))
    mpad[...] = jnp.where(lanes < WIDTH, outer, squares)

    def rows8(i):
        return pl.ds(pl.multiple_of(i * 8, 8), 8)

    for d in FAR_FIRST:
        to = at_t(d)
        send(
            mpad.at[rows8(to)], a2a.at[rows8(item)], a2a_s.at[d], a2a_r.at[t], r, to
        )
    for d in FAR_FIRST:
        to = at_y(d)
        send(
            mpad.at[rows8(to)], ly.at[rows8(y)], ly_s.at[d], ly_r.at[y], to * NZ + z, t
        )
    a2a[rows8(item), :] = mpad[rows8(t), :]
    ly[rows8(y), :] = mpad[rows8(y), :]

    for d in range(1, NT):
        src = at_t(d)
        remote(
            a2a.at[rows8(item_of(src))], a2a.at[rows8(item_of(src))], a2a_s.at[d], a2a_r.at[src], r, src
        ).wait_recv()
    lane8 = lax.broadcasted_iota(jnp.int32, (8, 2 * WIDTH), 1)
    sub8 = lax.broadcasted_iota(jnp.int32, (8, 2 * WIDTH), 0)
    for k in range(4):
        even = a2a[pl.ds(2 * k, 8, stride=8), :]
        odd = a2a[pl.ds(2 * k + 1, 8, stride=8), :]
        tile = jnp.where(lane8 < WIDTH, even, pltpu.roll(odd, WIDTH, 1))
        v_lu[:, k * 128 : (k + 1) * 128] = tile[0:4]
        v_ld[:, k * 128 : (k + 1) * 128] = tile[4:8]
        half = ra if k < 2 else rb
        half[z, y, :, (k % 2) * 128 : (k % 2 + 1) * 128] = tile

    for d in FAR_FIRST:
        to = at_z(d)
        send(
            ra.at[z, y], ra.at[z, y], p1a_s.at[d], p1a_r.at[z], y * NZ + to, t
        )
        to = at_y(d)
        send(
            rb.at[z, y], rb.at[z, y], p1b_s.at[d], p1b_r.at[y], to * NZ + z, t
        )


    for d in range(1, NY):
        src = at_y(d)
        remote(
            ly.at[rows8(src)], ly.at[rows8(src)], ly_s.at[d], ly_r.at[src], src * NZ + z, t
        ).wait_recv()
    for i in range(NZ):
        lz[i] = ly[pl.ds(i, 8, stride=8), :]
    for d in FAR_FIRST:
        to = at_z(d)
        slot = pl.ds(pl.multiple_of(item * 64 + z * 8, 8), 8)
        send(lz.at[to], lbuf.at[slot], lz_s.at[d], lz_r.at[z], y * NZ + to, t)
    lbuf[pl.ds(pl.multiple_of(item * 64 + z * 8, 8), 8), :] = lz[z]

    def block(h, c, k):
        if h == 0:
            return ra.at[pl.ds(SLOTS * c, SLOTS), at_y(k + NY)]
        return rb.at[at_z(k + NZ), pl.ds(SLOTS * c, SLOTS)]

    def pass_on(h, c, k, shift, kind):
        ref = block(h, c, k)
        dp = at_y(shift + NY) * NZ + z if h == 0 else y * NZ + at_z(shift + NZ)
        seen = k - shift if k - shift > -4 else 4
        base = (h * PIECES + c) * 8
        send(ref, ref, p2_s.at[base + kind], p2_r.at[base + seen + 3], dp, t)

    def arrived(h, c, k):
        ref = block(h, c, k)
        index = (h * PIECES + c) * 8 + k + 3
        remote(ref, ref, p2_s.at[index], p2_r.at[index], r, t).wait_recv()

    for c in range(PIECES):
        for h in range(2):
            for s in range(SLOTS * c, SLOTS * (c + 1)):

                @pl.when((z if h == 0 else y) != s)
                def _():
                    ref = ra.at[s, y] if h == 0 else rb.at[z, s]
                    sem = p1a_r if h == 0 else p1b_r
                    remote(ref, ref, p1a_s.at[0], sem.at[s], r, t).wait_recv()

            for kind, shift in enumerate((2, -2, 1, -1)):
                pass_on(h, c, 0, shift, kind)

    for d in range(1, NZ):
        src = at_z(d)
        slot = pl.ds(pl.multiple_of(item * 64 + src * 8, 8), 8)
        remote(lbuf.at[slot], lbuf.at[slot], lz_s.at[d], lz_r.at[src], r, t).wait_recv()

    def rows64(i):
        return pl.ds(pl.multiple_of(i * 64, 64), 64)

    for d in range(1, NT):
        send(lbuf.at[rows64(item)], lbuf.at[rows64(item)], lt_s.at[d], lt_r.at[t], r, at_t(d))

    for c in range(PIECES):
        for h in range(2):
            arrived(h, c, -2)
            if c % 2 == 0:
                pass_on(h, c, -2, 2, 6)
            pass_on(h, c, -2, 1, 4)
            arrived(h, c, 2)
            if c % 2 == 1:
                pass_on(h, c, 2, -2, 6)
            pass_on(h, c, 2, -1, 5)

    for m in range(NT):

        @pl.when(item != m)
        def _():
            remote(part.at[m], rs.at[t], rs_s.at[m], rs_r.at[t], r, m).wait_send()

    settle()
    for d in range(1, NT):
        src = at_t(d)
        remote(
            lbuf.at[rows64(item_of(src))], lbuf.at[rows64(item_of(src))], lt_s.at[d], lt_r.at[src], r, t
        ).wait_recv()
    tally = jnp.zeros((8, 2 * WIDTH), jnp.float32)
    for i in range(NY * NZ):
        tile = lbuf[pl.ds(i, 8, stride=64), :]
        tally = tally + tile
        low = jnp.where((sub8 < 4) & (lane8 < WIDTH), tile, 0.0)
        high = jnp.where((sub8 >= 4) & (lane8 >= WIDTH), pltpu.roll(tile, WIDTH, 1), 0.0)
        lp[i * 8 : (i + 1) * 8, :] = low + high
    tally = jnp.where(lane8 >= WIDTH, tally, 0.0)
    trace_up = jnp.sum(jnp.where(sub8 < 4, tally, 0.0)) / SEQS
    trace_dn = jnp.sum(jnp.where(sub8 >= 4, tally, 0.0)) / SEQS

    left = split(lp[...].T)
    row_ids = r * WIDTH + lax.broadcasted_iota(jnp.int32, (WIDTH, HALF), 0)
    col_ids = t * COLS + lax.broadcasted_iota(jnp.int32, (WIDTH, HALF), 1)
    for h in range(2):
        for c in range(PIECES):
            for k in (-1, 1, -3, 3, 4):
                arrived(h, c, k)
        half = ra if h == 0 else rb
        gram = times(left, split(half[...].reshape(8 * NY * NZ, HALF))) * (1.0 / SEQS)
        same = row_ids == col_ids + h * HALF
        cut = slice(h * HALF, (h + 1) * HALF)
        v_fu[:, cut] = gram[:WIDTH] + jnp.where(same, DAMPING * trace_up / FLAT, 0.0)
        v_fd[:, cut] = gram[WIDTH:] + jnp.where(same, DAMPING * trace_dn / FLAT, 0.0)

    settle()


def hand_over(*refs):
    given, taken, sems = refs[0:4], refs[4:8], refs[8]
    copies = [pltpu.make_async_copy(given[i], taken[i], sems.at[i]) for i in (2, 3, 0, 1)]
    for copy in copies:
        copy.start()
    for copy in copies:
        copy.wait()


def body(
    input_acts, hidden_acts, up_grads, output_grads, inner_up, outer_up, inner_down, outer_down
):
    operands = (
        input_acts,
        hidden_acts,
        up_grads,
        output_grads,
        inner_up,
        outer_up,
        inner_down,
        outer_down,
    )
    f32 = jnp.float32
    dma = pltpu.SemaphoreType.DMA
    shapes = [(NT // 2, COLS)] * 2 + [(WIDTH, COLS)] * 2
    out_shape = [jax.ShapeDtypeStruct(shape, f32) for shape in shapes]
    results = pl.pallas_call(
        kernel,
        out_shape=out_shape,
        in_specs=[pl.BlockSpec(memory_space=pltpu.HBM)] * 8,
        out_specs=[pl.BlockSpec(memory_space=pltpu.VMEM)] * 4,
        scratch_shapes=[pltpu.VMEM(a.shape, a.dtype) for a in operands]
        + [
            pltpu.VMEM((NT, LEN, 2 * WIDTH), f32),
            pltpu.VMEM((NT, LEN, 2 * WIDTH), f32),
            pltpu.VMEM((WIDTH, 2 * WIDTH), f32),
            pltpu.VMEM((8 * NT, 2 * WIDTH), f32),
            pltpu.VMEM((8 * NY, 2 * WIDTH), f32),
            pltpu.VMEM((NZ, NY, 2 * WIDTH), f32),
            pltpu.VMEM((NT * NZ * NY, 2 * WIDTH), f32),
            pltpu.VMEM((NT * NZ * NY, 2 * WIDTH), f32),
            pltpu.VMEM((NZ, NY, 8, HALF), f32),
            pltpu.VMEM((NZ, NY, 8, HALF), f32),
        ]
        + [dma((6 + 2 * (len(CUTS) - 1),))]
        + [dma((8,))] * 14
        + [dma((64,))] * 2,
        compiler_params=pltpu.CompilerParams(
            collective_id=0, has_side_effects=True, vmem_limit_bytes=54912 * 1024
        ),
        cost_estimate=pl.CostEstimate(
            flops=2 * 256 * 64 * 9216, bytes_accessed=6 * 1024 * 1024, transcendentals=0
        ),
    )(*operands)
    return pl.pallas_call(
        hand_over,
        out_shape=out_shape,
        in_specs=[pl.BlockSpec(memory_space=pltpu.VMEM)] * 4,
        out_specs=[pl.BlockSpec(memory_space=pltpu.HBM)] * 4,
        scratch_shapes=[dma((4,))],
        compiler_params=pltpu.CompilerParams(vmem_limit_bytes=1024 * 1024),
    )(*results)


def solution(mesh):
    split = P("dp", "tensor")
    basis = P(None, "tensor")
    return jax.shard_map(
        body,
        mesh=mesh,
        in_specs=(split,) * 4 + (basis,) * 4,
        out_specs=(split,) * 4,
        check_vma=False,
    )
```
